512 devices in a mesh: dp: 32 (over x, z), tensor: 16 (over y, core).
Axes of the slice: x: 4, y: 8, z: 8, core: 2. Of those that a mesh axis runs over, the one named last changes fastest.
Arguments:
- inputs: bfloat16 [16384, 5120], P('dp', 'tensor'), may hold values from -6 to 6
- out_grads: bfloat16 [2, 16384, 12800], P(None, 'dp', 'tensor'), may hold values from -0.046875 to 0.046875
- projector: bfloat16 [5120, 128], replicated, may hold values from -0.078125 to 0.078125
- first_moment: float32 [2, 128, 12800], P(None, 'dp', 'tensor'), may hold values from -4 to 4
- second_moment: float32 [2, 128, 12800], P(None, 'dp', 'tensor'), may hold values from 0.0001 to 0.01
Outputs:
- updates: bfloat16 [2, 5120, 12800], P(None, 'dp', 'tensor')
- new_first: float32 [2, 128, 12800], P(None, 'dp', 'tensor')
- new_second: float32 [2, 128, 12800], P(None, 'dp', 'tensor')
The draws below stay inside these ranges and needn't reach their ends.
All inputs are finite; a program needn't handle non-finite values.
Results may differ from the reference program's by a relative error of at most 0.0055.
Values may be sent and summed in bfloat16 or wider, within the bound.
No kernel may reach another device: no remote copies, remote signals or barrier semaphores. Data moves between devices by JAX's collectives and lax.ppermute only.
A program may use at most 64 MiB of HBM per device.

```python
import math
import jax
import jax.numpy as jnp

D = 5120
FF = 12800
RANK = 128
TOK_DEV = 512
TOKENS = 16384
N_DP = 32


def steps_of(key, extent, shards, smallest, largest):
    gain, own = 1.0, jax.random.fold_in(key, 6)
    for axis_at, parts in shards:
        heights = jnp.exp(jax.random.uniform(jax.random.fold_in(own, axis_at), (parts,), jnp.float32, smallest / len(shards), largest / len(shards)))
        gain = gain * jnp.repeat(heights, extent[axis_at] // parts).reshape([-1 if axis == axis_at else 1 for axis in range(len(extent))])
    return gain


def noise(rng, shape, width, limit, pieces=(), dtype=jnp.bfloat16):
    drawn = jax.random.normal(rng, shape, jnp.float32) * width
    if len(pieces) > 0:
        drawn = steps_of(rng, shape, pieces, -0.22, 0.18) * drawn
    return jnp.clip(drawn, min=-limit, max=limit).astype(dtype)


def setup_inputs(seed: int = 0) -> dict:
    splits = jax.random.split(jax.random.key(seed), 6)
    inputs = noise(splits[0], (TOKENS, D), 1.0, 6.0, ((0, 32), (1, 16)))
    out_grads = noise(splits[1], (2, TOKENS, FF), (TOK_DEV * N_DP) ** -0.5, 0.046875, ((1, 32), (2, 16)))
    projector = noise(splits[2], (D, RANK), D ** -0.5, 0.078125)
    first_moment = noise(splits[3], (2, RANK, FF), 0.3, 4.0, ((1, 32), (2, 16)), jnp.float32)
    second_moment = jnp.clip(jnp.exp(math.log(0.01) - 4.6051702 * jax.random.uniform(splits[4], (2, RANK, FF), jnp.float32) ** steps_of(splits[4], (2, RANK, FF), ((1, 32), (2, 16)), -0.2, 0.2)), 0.0001, 0.01)
    return dict(inputs=inputs, out_grads=out_grads, projector=projector, first_moment=first_moment, second_moment=second_moment)


def reference(inputs, out_grads, projector, first_moment, second_moment):
    low = jnp.dot(inputs, projector, preferred_element_type=jnp.float32).astype(jnp.bfloat16)
    low_t = low.T
    projected = jnp.stack([jnp.dot(low_t, out_grads[0], preferred_element_type=jnp.float32), jnp.dot(low_t, out_grads[1], preferred_element_type=jnp.float32)])
    new_first = 0.9 * first_moment + 0.1 * projected
    new_second = 0.999 * second_moment + 0.001 * projected * projected
    first_fix = 1.0 - 0.9 ** 10
    second_fix = 1.0 - 0.999 ** 10
    direction = (new_first / first_fix / (jnp.sqrt(new_second / second_fix) + 1e-08)).astype(jnp.bfloat16)
    updates = jnp.stack([jnp.dot(projector, direction[0], preferred_element_type=jnp.float32), jnp.dot(projector, direction[1], preferred_element_type=jnp.float32)]).astype(jnp.bfloat16)
    return (updates, new_first, new_second)
```

```python
import jax
import jax.numpy as jnp
from jax import lax
from jax.sharding import PartitionSpec as P


def exchange(blocks, axis):
    return lax.all_to_all(blocks, axis, 0, 0)


def gather(block, axis):
    return exchange(jnp.broadcast_to(block[None], (lax.axis_size(axis), *block.shape)), axis)


def per_device(inputs, out_grads, projector, first_moment, second_moment):
    tokens, feat_rows = inputs.shape
    n_grads, _, columns = out_grads.shape
    rank = projector.shape[1]
    n_dp, n_tensor = lax.axis_size("dp"), lax.axis_size("tensor")
    own_rows = lax.dynamic_slice_in_dim(
        projector, lax.axis_index("tensor") * feat_rows, feat_rows, 0
    )
    partial_sum = jnp.dot(inputs, own_rows, preferred_element_type=jnp.float32)
    parts = exchange(
        partial_sum.astype(jnp.bfloat16).reshape(n_tensor, tokens // n_tensor, rank), "tensor"
    )
    own_low = jnp.sum(parts.astype(jnp.float32), axis=0).astype(jnp.bfloat16)
    low = gather(own_low, "tensor").reshape(tokens, rank)
    projected = jnp.einsum("tr,ktc->krc", low, out_grads, preferred_element_type=jnp.float32)
    own_rank = rank // n_dp
    sent = projected.astype(jnp.bfloat16).reshape(n_grads, n_dp, own_rank, columns)
    sent = sent.transpose(1, 0, 2, 3).reshape(n_dp, n_grads * own_rank, columns)
    owned = jnp.sum(exchange(sent, "dp").astype(jnp.float32), axis=0)
    owned = owned.reshape(n_grads, own_rank, columns)
    new_first = 0.9 * first_moment + 0.1 * owned
    new_second = 0.999 * second_moment + 0.001 * owned * owned
    first_fix = 1.0 - 0.9**10
    second_fix = 1.0 - 0.999**10
    direction = (new_first / first_fix / (jnp.sqrt(new_second / second_fix) + 1e-08)).astype(
        jnp.bfloat16
    )
    every = gather(direction.reshape(n_grads * own_rank, columns), "dp")
    every = every.reshape(n_dp, n_grads, own_rank, columns).transpose(1, 0, 2, 3)
    every = every.reshape(n_grads, rank, columns)
    out_rows = projector.shape[0] // n_dp
    block_rows = lax.dynamic_slice_in_dim(projector, lax.axis_index("dp") * out_rows, out_rows, 0)
    expanded = jnp.einsum("dr,krc->kdc", block_rows, every, preferred_element_type=jnp.float32)
    return (expanded.astype(jnp.bfloat16), new_first, new_second)


def solution(mesh):
    return jax.shard_map(
        per_device,
        mesh=mesh,
        in_specs=(
            P("dp", "tensor"),
            P(None, "dp", "tensor"),
            P(),
            P(None, "dp", "tensor"),
            P(None, "dp", "tensor"),
        ),
        out_specs=(P(None, "dp", "tensor"), P(None, "dp", "tensor"), P(None, "dp", "tensor")),
        check_vma=False,
    )
```

```python
import jax
import jax.numpy as jnp
from jax import lax
from jax.experimental import pallas as pl
from jax.experimental.pallas import tpu as pltpu
from jax.sharding import PartitionSpec as P

FIRST_FIX = 1.0 - 0.9**10
SECOND_FIX = 1.0 - 0.999**10
PARAMS = pltpu.CompilerParams(vmem_limit_bytes=16 * 1024 * 1024)
VMEM = pl.BlockSpec(memory_space=pltpu.VMEM)
HBM = pl.BlockSpec(memory_space=pltpu.HBM)


def exchange(blocks, axis):
    return lax.all_to_all(blocks, axis, 0, 0)


def cost(flops, nbytes):
    return pl.CostEstimate(flops=flops, bytes_accessed=nbytes, transcendentals=0)


def low_kernel(x_ref, p_ref, parts_ref, rows_ref, x_buf, p_buf, sems):
    n, height, tokens = parts_ref.shape
    feats, out_rows = x_ref.shape[0], rows_ref.shape[0]
    own = pl.multiple_of(lax.axis_index("tensor") * feats, 16)
    block = pl.multiple_of(lax.axis_index("dp") * out_rows, 16)
    copies = (
        pltpu.make_async_copy(p_ref.at[pl.ds(own, feats)], p_buf, sems.at[0]),
        pltpu.make_async_copy(x_ref, x_buf, sems.at[1]),
        pltpu.make_async_copy(p_ref.at[pl.ds(block, out_rows)], rows_ref, sems.at[2]),
    )
    for copy in copies:
        copy.start()
    copies[0].wait()
    copies[1].wait()
    partial_sum = lax.dot_general(
        p_buf[...], x_buf[...], (((0,), (0,)), ((), ())), preferred_element_type=jnp.float32
    )
    parts_ref[...] = partial_sum.astype(parts_ref.dtype).reshape(n, height, tokens)
    copies[2].wait()


def low_parts(inputs, projector, n_tensor, n_dp):
    tokens, feats = inputs.shape
    width, rank = projector.shape
    bf16 = jnp.bfloat16
    return pl.pallas_call(
        low_kernel,
        out_shape=(
            pltpu.VMEM((n_tensor, rank // n_tensor, tokens), bf16),
            pltpu.VMEM((width // n_dp, rank), bf16),
        ),
        in_specs=[HBM, HBM],
        out_specs=[VMEM, VMEM],
        scratch_shapes=[
            pltpu.VMEM((feats, tokens), bf16),
            pltpu.VMEM((feats, rank), bf16),
            pltpu.SemaphoreType.DMA((3,)),
        ],
        compiler_params=PARAMS,
        cost_estimate=cost(2 * tokens * feats * rank, 2 * feats * (tokens + rank)),
    )(inputs.T, projector)


def halves(shape):
    return lax.broadcasted_iota(jnp.int32, shape, 1) < shape[1] // 2


def project_kernel(low_ref, grads_ref, out_ref):
    groups, height, tokens = low_ref.shape
    columns = grads_ref.shape[1]
    low = low_ref[...].reshape(groups * height, tokens)
    gate, up = (
        lax.dot_general(
            low, grads_ref[k], (((1,), (1,)), ((), ())), preferred_element_type=jnp.float32
        ).reshape(groups, height, columns)
        for k in range(2)
    )
    upper = halves(gate.shape)
    turn = height // 2
    out_ref[:, 0] = jnp.where(upper, gate, pltpu.roll(up, turn, 1)).astype(out_ref.dtype)
    out_ref[:, 1] = jnp.where(upper, pltpu.roll(gate, turn, 1), up).astype(out_ref.dtype)


def project(low, grads):
    groups, height, tokens = low.shape
    columns = grads.shape[1]
    return pl.pallas_call(
        project_kernel,
        out_shape=pltpu.VMEM((groups, 2, height, columns), jnp.bfloat16),
        in_specs=[VMEM, VMEM],
        out_specs=VMEM,
        compiler_params=PARAMS,
        cost_estimate=cost(4 * groups * height * tokens * columns, 4 * tokens * columns),
    )(low, grads)


def adam_kernel(parts_ref, first_ref, second_ref, out_ref, new_first_ref, new_second_ref):
    own = jnp.sum(parts_ref[...].astype(jnp.float32), axis=0)
    n_grads, height, _ = first_ref.shape
    direction = []
    for k in range(n_grads):
        projected = own[k * height : (k + 1) * height]
        first = 0.9 * first_ref[k] + 0.1 * projected
        second = 0.999 * second_ref[k] + 0.001 * projected * projected
        new_first_ref[k] = first
        new_second_ref[k] = second
        direction.append(first / FIRST_FIX / (jnp.sqrt(second / SECOND_FIX) + 1e-08))
    direction = jnp.concatenate(direction, axis=0).astype(out_ref.dtype)
    out_ref[...] = jnp.broadcast_to(direction[None], out_ref.shape)


def adam(parts, first, second):
    return pl.pallas_call(
        adam_kernel,
        out_shape=(
            pltpu.VMEM(parts.shape, jnp.bfloat16),
            pltpu.VMEM(first.shape, jnp.float32),
            pltpu.VMEM(second.shape, jnp.float32),
        ),
        in_specs=[VMEM] * 3,
        out_specs=[VMEM] * 3,
        compiler_params=PARAMS,
        cost_estimate=cost(parts.size, 4 * parts.size),
    )(parts, first, second)


def expand_kernel(
    rows_ref, dirs_ref, first_ref, second_ref, out_ref, new_first_ref, new_second_ref, buf, sems
):
    pairs, _, height, columns = dirs_ref.shape
    copies = [
        pltpu.make_async_copy(first_ref, new_first_ref, sems.at[2]),
        pltpu.make_async_copy(second_ref, new_second_ref, sems.at[3]),
    ]
    for copy in copies:
        copy.start()
    even = dirs_ref[:, 0].astype(jnp.float32)
    odd = dirs_ref[:, 1].astype(jnp.float32)
    upper = halves(even.shape)
    turn = height // 2
    ordered = (
        jnp.where(upper, even, pltpu.roll(odd, turn, 1)),
        jnp.where(upper, pltpu.roll(even, turn, 1), odd),
    )
    for k in range(2):
        direction = ordered[k].astype(jnp.bfloat16).reshape(pairs * height, columns)
        update = jnp.dot(rows_ref[...], direction, preferred_element_type=jnp.float32)
        buf[k] = update.astype(buf.dtype)
        copies.append(pltpu.make_async_copy(buf.at[k], out_ref.at[k], sems.at[k]))
        copies[-1].start()
    for copy in copies:
        copy.wait()


def expand(rows, dirs, first, second):
    out_rows, rank = rows.shape
    columns = dirs.shape[-1]
    shape = (2, out_rows, columns)
    return pl.pallas_call(
        expand_kernel,
        out_shape=(
            pltpu.HBM(shape, jnp.bfloat16),
            pltpu.HBM(first.shape, first.dtype),
            pltpu.HBM(second.shape, second.dtype),
        ),
        in_specs=[VMEM] * 4,
        out_specs=[HBM] * 3,
        scratch_shapes=[pltpu.VMEM(shape, jnp.bfloat16), pltpu.SemaphoreType.DMA((4,))],
        compiler_params=PARAMS,
        cost_estimate=cost(4 * out_rows * rank * columns, 4 * out_rows * columns),
    )(rows, dirs, first, second)


def per_device(inputs, out_grads, projector, first_moment, second_moment):
    n_dp, n_tensor = lax.axis_size("dp"), lax.axis_size("tensor")
    columns = out_grads.shape[2]
    parts, rows = low_parts(inputs, projector, n_tensor, n_dp)
    parts = exchange(parts, "tensor")
    own_low = jnp.sum(parts.astype(jnp.float32), axis=0).astype(jnp.bfloat16)
    low = exchange(jnp.broadcast_to(own_low[None], parts.shape), "tensor")
    sent = project(low, out_grads.transpose(0, 2, 1))
    received = exchange(sent.reshape(n_dp, -1, columns), "dp")
    direction, new_first, new_second = adam(received, first_moment, second_moment)
    every = exchange(direction, "dp").reshape(sent.shape)
    return expand(rows, every, new_first, new_second)


def solution(mesh):
    return jax.shard_map(
        per_device,
        mesh=mesh,
        in_specs=(
            P("dp", "tensor"),
            P(None, "dp", "tensor"),
            P(),
            P(None, "dp", "tensor"),
            P(None, "dp", "tensor"),
        ),
        out_specs=(P(None, "dp", "tensor"), P(None, "dp", "tensor"), P(None, "dp", "tensor")),
        check_vma=False,
    )
```

```python
import jax
import jax.numpy as jnp
from jax import lax
from jax.experimental import pallas as pl
from jax.experimental.pallas import tpu as pltpu
from jax.sharding import PartitionSpec as P

FIRST_FIX = 1.0 - 0.9**10
SECOND_FIX = 1.0 - 0.999**10
PARAMS = pltpu.CompilerParams(vmem_limit_bytes=16 * 1024 * 1024)
VMEM = pl.BlockSpec(memory_space=pltpu.VMEM)
HBM = pl.BlockSpec(memory_space=pltpu.HBM)


def exchange(blocks, axis):
    return lax.all_to_all(blocks, axis, 0, 0)


def cost(flops, nbytes):
    return pl.CostEstimate(flops=flops, bytes_accessed=nbytes, transcendentals=0)


def low_kernel(x_ref, p_ref, parts_ref, rows_ref, x_buf, p_buf, sems):
    n, height, tokens = parts_ref.shape
    feats, out_rows = x_ref.shape[0], rows_ref.shape[0]
    own = pl.multiple_of(lax.axis_index("tensor") * feats, 16)
    block = pl.multiple_of(lax.axis_index("dp") * out_rows, 16)
    copies = (
        pltpu.make_async_copy(p_ref.at[pl.ds(own, feats)], p_buf, sems.at[0]),
        pltpu.make_async_copy(x_ref, x_buf, sems.at[1]),
        pltpu.make_async_copy(p_ref.at[pl.ds(block, out_rows)], rows_ref, sems.at[2]),
    )
    for copy in copies:
        copy.start()
    copies[0].wait()
    copies[1].wait()
    partial_sum = lax.dot_general(
        p_buf[...], x_buf[...], (((0,), (0,)), ((), ())), preferred_element_type=jnp.float32
    )
    parts_ref[...] = partial_sum.astype(parts_ref.dtype).reshape(n, height, tokens)
    copies[2].wait()


def low_parts(inputs, projector, n_tensor, n_dp):
    tokens, feats = inputs.shape
    width, rank = projector.shape
    bf16 = jnp.bfloat16
    return pl.pallas_call(
        low_kernel,
        out_shape=(
            pltpu.VMEM((n_tensor, rank // n_tensor, tokens), bf16),
            pltpu.VMEM((width // n_dp, rank), bf16),
        ),
        in_specs=[HBM, HBM],
        out_specs=[VMEM, VMEM],
        scratch_shapes=[
            pltpu.VMEM((feats, tokens), bf16),
            pltpu.VMEM((feats, rank), bf16),
            pltpu.SemaphoreType.DMA((3,)),
        ],
        compiler_params=PARAMS,
        cost_estimate=cost(2 * tokens * feats * rank, 2 * feats * (tokens + rank)),
    )(
        pltpu.with_memory_space_constraint(inputs.T, pltpu.HBM),
        pltpu.with_memory_space_constraint(projector, pltpu.HBM),
    )


def halves(shape):
    return lax.broadcasted_iota(jnp.int32, shape, 1) < shape[1] // 2


def project_kernel(low_ref, grads_ref, out_ref):
    groups, height, tokens = low_ref.shape
    columns = grads_ref.shape[1]
    low = low_ref[...].reshape(groups * height, tokens)
    gate, up = (
        lax.dot_general(
            low, grads_ref[k], (((1,), (1,)), ((), ())), preferred_element_type=jnp.float32
        ).reshape(groups, height, columns)
        for k in range(2)
    )
    upper = halves(gate.shape)
    turn = height // 2
    out_ref[:, 0] = jnp.where(upper, gate, pltpu.roll(up, turn, 1)).astype(out_ref.dtype)
    out_ref[:, 1] = jnp.where(upper, pltpu.roll(gate, turn, 1), up).astype(out_ref.dtype)


def project(low, grads):
    groups, height, tokens = low.shape
    columns = grads.shape[1]
    return pl.pallas_call(
        project_kernel,
        out_shape=pltpu.VMEM((groups, 2, height, columns), jnp.bfloat16),
        in_specs=[VMEM, VMEM],
        out_specs=VMEM,
        compiler_params=PARAMS,
        cost_estimate=cost(4 * groups * height * tokens * columns, 4 * tokens * columns),
    )(low, grads)


def adam_kernel(parts_ref, first_ref, second_ref, out_ref, new_first_ref, new_second_ref):
    own = jnp.sum(parts_ref[...].astype(jnp.float32), axis=0)
    n_grads, height, _ = first_ref.shape
    direction = []
    for k in range(n_grads):
        projected = own[k * height : (k + 1) * height]
        first = 0.9 * first_ref[k] + 0.1 * projected
        second = 0.999 * second_ref[k] + 0.001 * projected * projected
        new_first_ref[k] = first
        new_second_ref[k] = second
        direction.append(first / FIRST_FIX / (jnp.sqrt(second / SECOND_FIX) + 1e-08))
    direction = jnp.concatenate(direction, axis=0).astype(out_ref.dtype)
    out_ref[...] = jnp.broadcast_to(direction[None], out_ref.shape)


def adam(parts, first, second):
    return pl.pallas_call(
        adam_kernel,
        out_shape=(
            pltpu.VMEM(parts.shape, jnp.bfloat16),
            pltpu.VMEM(first.shape, jnp.float32),
            pltpu.VMEM(second.shape, jnp.float32),
        ),
        in_specs=[VMEM] * 3,
        out_specs=[VMEM] * 3,
        compiler_params=PARAMS,
        cost_estimate=cost(parts.size, 4 * parts.size),
    )(parts, first, second)


def expand_kernel(
    rows_ref, dirs_ref, first_ref, second_ref, out_ref, new_first_ref, new_second_ref, buf, sems
):
    pairs, _, height, columns = dirs_ref.shape
    copies = [
        pltpu.make_async_copy(first_ref, new_first_ref, sems.at[2]),
        pltpu.make_async_copy(second_ref, new_second_ref, sems.at[3]),
    ]
    for copy in copies:
        copy.start()
    even = dirs_ref[:, 0].astype(jnp.float32)
    odd = dirs_ref[:, 1].astype(jnp.float32)
    upper = halves(even.shape)
    turn = height // 2
    ordered = (
        jnp.where(upper, even, pltpu.roll(odd, turn, 1)),
        jnp.where(upper, pltpu.roll(even, turn, 1), odd),
    )
    for k in range(2):
        direction = ordered[k].astype(jnp.bfloat16).reshape(pairs * height, columns)
        update = jnp.dot(rows_ref[...], direction, preferred_element_type=jnp.float32)
        buf[k] = update.astype(buf.dtype)
        copies.append(pltpu.make_async_copy(buf.at[k], out_ref.at[k], sems.at[k]))
        copies[-1].start()
    for copy in copies:
        copy.wait()


def expand(rows, dirs, first, second):
    out_rows, rank = rows.shape
    columns = dirs.shape[-1]
    shape = (2, out_rows, columns)
    return pl.pallas_call(
        expand_kernel,
        out_shape=(
            pltpu.HBM(shape, jnp.bfloat16),
            pltpu.HBM(first.shape, first.dtype),
            pltpu.HBM(second.shape, second.dtype),
        ),
        in_specs=[VMEM] * 4,
        out_specs=[HBM] * 3,
        scratch_shapes=[pltpu.VMEM(shape, jnp.bfloat16), pltpu.SemaphoreType.DMA((4,))],
        compiler_params=PARAMS,
        cost_estimate=cost(4 * out_rows * rank * columns, 4 * out_rows * columns),
    )(rows, dirs, first, second)


def per_device(inputs, out_grads, projector, first_moment, second_moment):
    n_dp, n_tensor = lax.axis_size("dp"), lax.axis_size("tensor")
    columns = out_grads.shape[2]
    parts, rows = low_parts(inputs, projector, n_tensor, n_dp)
    parts = exchange(parts, "tensor")
    own_low = jnp.sum(parts.astype(jnp.float32), axis=0).astype(jnp.bfloat16)
    low = exchange(jnp.broadcast_to(own_low[None], parts.shape), "tensor")
    sent = project(low, out_grads.transpose(0, 2, 1))
    received = exchange(sent.reshape(n_dp, -1, columns), "dp")
    direction, new_first, new_second = adam(received, first_moment, second_moment)
    every = exchange(direction, "dp").reshape(sent.shape)
    return expand(rows, every, new_first, new_second)


def solution(mesh):
    return jax.shard_map(
        per_device,
        mesh=mesh,
        in_specs=(
            P("dp", "tensor"),
            P(None, "dp", "tensor"),
            P(),
            P(None, "dp", "tensor"),
            P(None, "dp", "tensor"),
        ),
        out_specs=(P(None, "dp", "tensor"), P(None, "dp", "tensor"), P(None, "dp", "tensor")),
        check_vma=False,
    )
```

```python
import jax
import jax.numpy as jnp
from jax import lax
from jax.experimental import pallas as pl
from jax.experimental.pallas import tpu as pltpu
from jax.sharding import PartitionSpec as P

FIRST_FIX = 1.0 - 0.9**10
SECOND_FIX = 1.0 - 0.999**10
PARAMS = pltpu.CompilerParams(vmem_limit_bytes=16 * 1024 * 1024)
CHIPS_Z = 8
CORES = 2
SMEM = pl.BlockSpec(memory_space=pltpu.SMEM)
VMEM = pl.BlockSpec(memory_space=pltpu.VMEM)
HBM = pl.BlockSpec(memory_space=pltpu.HBM)


def exchange(blocks, axis, groups=None):
    return lax.all_to_all(blocks, axis, 0, 0, axis_index_groups=groups)


def rows_sum(parts):
    return jnp.sum(parts.astype(jnp.float32), axis=0)


def scatter_at_once(sent):
    return rows_sum(exchange(sent, "dp"))


def scatter_by_axis(sent):
    n_dp, height, columns = sent.shape
    n_x = n_dp // CHIPS_Z
    lines = [[x * CHIPS_Z + z for x in range(n_x)] for z in range(CHIPS_Z)]
    planes = [[x * CHIPS_Z + z for z in range(CHIPS_Z)] for x in range(n_x)]
    along_x = exchange(sent.reshape(n_x, CHIPS_Z * height, columns), "dp", lines)
    own_plane = rows_sum(along_x).astype(sent.dtype).reshape(CHIPS_Z, height, columns)
    return rows_sum(exchange(own_plane, "dp", planes))


def cost(flops, nbytes):
    return pl.CostEstimate(flops=flops, bytes_accessed=nbytes, transcendentals=0)


def low_kernel(first_core_ref, x_ref, p_ref, parts_ref, rows_ref, x_buf, p_buf, sems):
    n, height, tokens = parts_ref.shape
    feats, out_rows = x_ref.shape[0], rows_ref.shape[0]
    chip = lax.axis_index("tensor") // CORES
    own = pl.multiple_of((chip * CORES + 1 - first_core_ref[0]) * feats, 16)
    block = pl.multiple_of(lax.axis_index("dp") * out_rows, 16)
    copies = (
        pltpu.make_async_copy(p_ref.at[pl.ds(own, feats)], p_buf, sems.at[0]),
        pltpu.make_async_copy(x_ref, x_buf, sems.at[1]),
        pltpu.make_async_copy(p_ref.at[pl.ds(block, out_rows)], rows_ref, sems.at[2]),
    )
    for copy in copies:
        copy.start()
    copies[0].wait()
    copies[1].wait()
    partial_sum = lax.dot_general(
        p_buf[...], x_buf[...], (((0,), (0,)), ((), ())), preferred_element_type=jnp.float32
    )
    parts_ref[...] = partial_sum.astype(parts_ref.dtype).reshape(n, height, tokens)
    copies[2].wait()


def low_parts(first_core, inputs, projector, n_tensor, n_dp):
    tokens, feats = inputs.shape
    width, rank = projector.shape
    bf16 = jnp.bfloat16
    return pl.pallas_call(
        low_kernel,
        out_shape=(
            pltpu.VMEM((n_tensor, rank // n_tensor, tokens), bf16),
            pltpu.VMEM((width // n_dp, rank), bf16),
        ),
        in_specs=[SMEM, HBM, HBM],
        out_specs=[VMEM, VMEM],
        scratch_shapes=[
            pltpu.VMEM((feats, tokens), bf16),
            pltpu.VMEM((feats, rank), bf16),
            pltpu.SemaphoreType.DMA((3,)),
        ],
        compiler_params=PARAMS,
        cost_estimate=cost(2 * tokens * feats * rank, 2 * feats * (tokens + rank)),
    )(
        first_core.astype(jnp.int32).reshape(1),
        pltpu.with_memory_space_constraint(inputs.T, pltpu.HBM),
        pltpu.with_memory_space_constraint(projector, pltpu.HBM),
    )


def spread_kernel(parts_ref, out_ref):
    own = jnp.sum(parts_ref[...].astype(jnp.float32), axis=0).astype(out_ref.dtype)
    out_ref[...] = jnp.broadcast_to(own[None], out_ref.shape)


def spread(parts):
    return pl.pallas_call(
        spread_kernel,
        out_shape=pltpu.VMEM(parts.shape, parts.dtype),
        in_specs=[VMEM],
        out_specs=VMEM,
        compiler_params=PARAMS,
        cost_estimate=cost(parts.size, 4 * parts.size),
    )(parts)


def halves(shape):
    return lax.broadcasted_iota(jnp.int32, shape, 1) < shape[1] // 2


def project_kernel(low_ref, grads_ref, out_ref):
    groups, height, tokens = low_ref.shape
    columns = grads_ref.shape[1]
    low = low_ref[...].reshape(groups * height, tokens)
    gate, up = (
        lax.dot_general(
            low, grads_ref[k], (((1,), (1,)), ((), ())), preferred_element_type=jnp.float32
        ).reshape(groups, height, columns)
        for k in range(2)
    )
    upper = halves(gate.shape)
    turn = height // 2
    out_ref[:, 0] = jnp.where(upper, gate, pltpu.roll(up, turn, 1)).astype(out_ref.dtype)
    out_ref[:, 1] = jnp.where(upper, pltpu.roll(gate, turn, 1), up).astype(out_ref.dtype)


def project(low, grads):
    groups, height, tokens = low.shape
    columns = grads.shape[1]
    return pl.pallas_call(
        project_kernel,
        out_shape=pltpu.VMEM((groups, 2, height, columns), jnp.bfloat16),
        in_specs=[VMEM, VMEM],
        out_specs=VMEM,
        compiler_params=PARAMS,
        cost_estimate=cost(4 * groups * height * tokens * columns, 4 * tokens * columns),
    )(low, grads)


def adam_kernel(own_ref, first_ref, second_ref, out_ref, new_first_ref, new_second_ref):
    n_grads, height, _ = first_ref.shape
    direction = []
    for k in range(n_grads):
        projected = own_ref[k * height : (k + 1) * height]
        first = 0.9 * first_ref[k] + 0.1 * projected
        second = 0.999 * second_ref[k] + 0.001 * projected * projected
        new_first_ref[k] = first
        new_second_ref[k] = second
        direction.append(first / FIRST_FIX / (jnp.sqrt(second / SECOND_FIX) + 1e-08))
    direction = jnp.concatenate(direction, axis=0).astype(out_ref.dtype)
    out_ref[...] = jnp.broadcast_to(direction[None], out_ref.shape)


def adam(own, first, second, n_dp):
    return pl.pallas_call(
        adam_kernel,
        out_shape=(
            pltpu.VMEM((n_dp, *own.shape), jnp.bfloat16),
            pltpu.VMEM(first.shape, jnp.float32),
            pltpu.VMEM(second.shape, jnp.float32),
        ),
        in_specs=[VMEM] * 3,
        out_specs=[VMEM] * 3,
        compiler_params=PARAMS,
        cost_estimate=cost(20 * own.size, 2 * n_dp * own.size),
    )(own, first, second)


def expand_kernel(
    rows_ref, dirs_ref, first_ref, second_ref, out_ref, new_first_ref, new_second_ref, buf, sems
):
    pairs, _, height, columns = dirs_ref.shape
    copies = [
        pltpu.make_async_copy(first_ref, new_first_ref, sems.at[2]),
        pltpu.make_async_copy(second_ref, new_second_ref, sems.at[3]),
    ]
    for copy in copies:
        copy.start()
    even = dirs_ref[:, 0].astype(jnp.float32)
    odd = dirs_ref[:, 1].astype(jnp.float32)
    upper = halves(even.shape)
    turn = height // 2
    ordered = (
        jnp.where(upper, even, pltpu.roll(odd, turn, 1)),
        jnp.where(upper, pltpu.roll(even, turn, 1), odd),
    )
    for k in range(2):
        direction = ordered[k].astype(jnp.bfloat16).reshape(pairs * height, columns)
        update = jnp.dot(rows_ref[...], direction, preferred_element_type=jnp.float32)
        buf[k] = update.astype(buf.dtype)
        copies.append(pltpu.make_async_copy(buf.at[k], out_ref.at[k], sems.at[k]))
        copies[-1].start()
    for copy in copies:
        copy.wait()


def expand(rows, dirs, first, second):
    out_rows, rank = rows.shape
    columns = dirs.shape[-1]
    shape = (2, out_rows, columns)
    return pl.pallas_call(
        expand_kernel,
        out_shape=(
            pltpu.HBM(shape, jnp.bfloat16),
            pltpu.HBM(first.shape, first.dtype),
            pltpu.HBM(second.shape, second.dtype),
        ),
        in_specs=[VMEM] * 4,
        out_specs=[HBM] * 3,
        scratch_shapes=[pltpu.VMEM(shape, jnp.bfloat16), pltpu.SemaphoreType.DMA((4,))],
        compiler_params=PARAMS,
        cost_estimate=cost(4 * out_rows * rank * columns, 4 * out_rows * columns),
    )(rows, dirs, first, second)


def per_device(inputs, out_grads, projector, first_moment, second_moment):
    n_dp, n_tensor = lax.axis_size("dp"), lax.axis_size("tensor")
    columns = out_grads.shape[2]
    first_core = lax.axis_index("tensor") % CORES == 0
    parts, rows = low_parts(first_core, inputs, projector, n_tensor, n_dp)
    low = exchange(spread(exchange(parts, "tensor")), "tensor")
    sent = project(low, out_grads.transpose(0, 2, 1))
    own = lax.cond(
        first_core,
        scatter_by_axis,
        scatter_at_once,
        sent.reshape(n_dp, -1, columns),
    )
    direction, new_first, new_second = adam(own, first_moment, second_moment, n_dp)
    every = exchange(direction, "dp").reshape(sent.shape)
    return expand(rows, every, new_first, new_second)


def solution(mesh):
    return jax.shard_map(
        per_device,
        mesh=mesh,
        in_specs=(
            P("dp", "tensor"),
            P(None, "dp", "tensor"),
            P(),
            P(None, "dp", "tensor"),
            P(None, "dp", "tensor"),
        ),
        out_specs=(P(None, "dp", "tensor"), P(None, "dp", "tensor"), P(None, "dp", "tensor")),
        check_vma=False,
    )
```

```python
import jax
import jax.numpy as jnp
from jax import lax
from jax.experimental import pallas as pl
from jax.experimental.pallas import tpu as pltpu
from jax.sharding import PartitionSpec as P

FIRST_FIX = 1.0 - 0.9**10
SECOND_FIX = 1.0 - 0.999**10
PARAMS = pltpu.CompilerParams(vmem_limit_bytes=16 * 1024 * 1024)
CHIPS_Z = 8
HUB_X, HUB_Z, HUB_Y = 2, 4, 4
CORES = 2
SMEM = pl.BlockSpec(memory_space=pltpu.SMEM)
VMEM = pl.BlockSpec(memory_space=pltpu.VMEM)
HBM = pl.BlockSpec(memory_space=pltpu.HBM)


def exchange(blocks, axis, groups=None):
    return lax.all_to_all(blocks, axis, 0, 0, axis_index_groups=groups)


def dp_order(n_dp):
    hub = HUB_X * CHIPS_Z + HUB_Z
    return [[at ^ hub for at in range(n_dp)]]


def tensor_order(n_tensor):
    return [[at ^ (HUB_Y * CORES) for at in range(n_tensor)]]


def rows_sum(parts):
    return jnp.sum(parts.astype(jnp.float32), axis=0)


def scatter_at_once(sent):
    return rows_sum(exchange(sent, "dp", dp_order(sent.shape[0])))


def scatter_by_axis(sent):
    n_dp, height, columns = sent.shape
    n_x = n_dp // CHIPS_Z
    lines = [[(x ^ HUB_X) * CHIPS_Z + z for x in range(n_x)] for z in range(CHIPS_Z)]
    planes = [[x * CHIPS_Z + (z ^ HUB_Z) for z in range(CHIPS_Z)] for x in range(n_x)]
    along_x = exchange(sent.reshape(n_x, CHIPS_Z * height, columns), "dp", lines)
    own_plane = rows_sum(along_x).astype(sent.dtype).reshape(CHIPS_Z, height, columns)
    return rows_sum(exchange(own_plane, "dp", planes))


def cost(flops, nbytes):
    return pl.CostEstimate(flops=flops, bytes_accessed=nbytes, transcendentals=0)


def low_kernel(first_core_ref, x_ref, p_ref, parts_ref, rows_ref, x_buf, p_buf, sems):
    n, height, tokens = parts_ref.shape
    feats, out_rows = x_ref.shape[0], rows_ref.shape[0]
    chip = lax.axis_index("tensor") // CORES
    own = pl.multiple_of((chip * CORES + 1 - first_core_ref[0]) * feats, 16)
    block = pl.multiple_of(lax.axis_index("dp") * out_rows, 16)
    copies = (
        pltpu.make_async_copy(p_ref.at[pl.ds(own, feats)], p_buf, sems.at[0]),
        pltpu.make_async_copy(x_ref, x_buf, sems.at[1]),
        pltpu.make_async_copy(p_ref.at[pl.ds(block, out_rows)], rows_ref, sems.at[2]),
    )
    for copy in copies:
        copy.start()
    copies[0].wait()
    copies[1].wait()
    partial_sum = lax.dot_general(
        p_buf[...], x_buf[...], (((0,), (0,)), ((), ())), preferred_element_type=jnp.float32
    )
    parts_ref[...] = partial_sum.astype(parts_ref.dtype).reshape(n, height, tokens)
    copies[2].wait()


def low_parts(first_core, inputs, projector, n_tensor, n_dp):
    tokens, feats = inputs.shape
    width, rank = projector.shape
    bf16 = jnp.bfloat16
    return pl.pallas_call(
        low_kernel,
        out_shape=(
            pltpu.VMEM((n_tensor, rank // n_tensor, tokens), bf16),
            pltpu.VMEM((width // n_dp, rank), bf16),
        ),
        in_specs=[SMEM, HBM, HBM],
        out_specs=[VMEM, VMEM],
        scratch_shapes=[
            pltpu.VMEM((feats, tokens), bf16),
            pltpu.VMEM((feats, rank), bf16),
            pltpu.SemaphoreType.DMA((3,)),
        ],
        compiler_params=PARAMS,
        cost_estimate=cost(2 * tokens * feats * rank, 2 * feats * (tokens + rank)),
    )(
        first_core.astype(jnp.int32).reshape(1),
        pltpu.with_memory_space_constraint(inputs.T, pltpu.HBM),
        pltpu.with_memory_space_constraint(projector, pltpu.HBM),
    )


def spread_kernel(parts_ref, out_ref):
    own = jnp.sum(parts_ref[...].astype(jnp.float32), axis=0).astype(out_ref.dtype)
    out_ref[...] = jnp.broadcast_to(own[None], out_ref.shape)


def spread(parts):
    return pl.pallas_call(
        spread_kernel,
        out_shape=pltpu.VMEM(parts.shape, parts.dtype),
        in_specs=[VMEM],
        out_specs=VMEM,
        compiler_params=PARAMS,
        cost_estimate=cost(parts.size, 4 * parts.size),
    )(parts)


def pair_at(pair):
    return pair ^ ((HUB_X * CHIPS_Z + HUB_Z) // 2)


def halves(shape):
    return lax.broadcasted_iota(jnp.int32, shape, 1) < shape[1] // 2


def project_kernel(low_ref, grads_ref, out_ref):
    groups, height, tokens = low_ref.shape
    columns = grads_ref.shape[1]
    low = low_ref[...].reshape(groups * height, tokens)
    gate, up = (
        lax.dot_general(
            low, grads_ref[k], (((1,), (1,)), ((), ())), preferred_element_type=jnp.float32
        ).reshape(groups, height, columns)
        for k in range(2)
    )
    upper = halves(gate.shape)
    turn = height // 2
    even = jnp.where(upper, gate, pltpu.roll(up, turn, 1)).astype(out_ref.dtype)
    odd = jnp.where(upper, pltpu.roll(gate, turn, 1), up).astype(out_ref.dtype)
    for pair in range(groups):
        out_ref[pair_at(pair), 0] = even[pair]
        out_ref[pair_at(pair), 1] = odd[pair]


def project(low, grads):
    groups, height, tokens = low.shape
    columns = grads.shape[1]
    return pl.pallas_call(
        project_kernel,
        out_shape=pltpu.VMEM((groups, 2, height, columns), jnp.bfloat16),
        in_specs=[VMEM, VMEM],
        out_specs=VMEM,
        compiler_params=PARAMS,
        cost_estimate=cost(4 * groups * height * tokens * columns, 4 * tokens * columns),
    )(low, grads)


def adam_kernel(own_ref, first_ref, second_ref, out_ref, new_first_ref, new_second_ref):
    n_grads, height, _ = first_ref.shape
    direction = []
    for k in range(n_grads):
        projected = own_ref[k * height : (k + 1) * height]
        first = 0.9 * first_ref[k] + 0.1 * projected
        second = 0.999 * second_ref[k] + 0.001 * projected * projected
        new_first_ref[k] = first
        new_second_ref[k] = second
        direction.append(first / FIRST_FIX / (jnp.sqrt(second / SECOND_FIX) + 1e-08))
    direction = jnp.concatenate(direction, axis=0).astype(out_ref.dtype)
    out_ref[...] = jnp.broadcast_to(direction[None], out_ref.shape)


def adam(own, first, second, n_dp):
    return pl.pallas_call(
        adam_kernel,
        out_shape=(
            pltpu.VMEM((n_dp, *own.shape), jnp.bfloat16),
            pltpu.VMEM(first.shape, jnp.float32),
            pltpu.VMEM(second.shape, jnp.float32),
        ),
        in_specs=[VMEM] * 3,
        out_specs=[VMEM] * 3,
        compiler_params=PARAMS,
        cost_estimate=cost(20 * own.size, 2 * n_dp * own.size),
    )(own, first, second)


def expand_kernel(
    rows_ref, dirs_ref, first_ref, second_ref, out_ref, new_first_ref, new_second_ref, buf, sems
):
    pairs, _, height, columns = dirs_ref.shape
    copies = [
        pltpu.make_async_copy(first_ref, new_first_ref, sems.at[2]),
        pltpu.make_async_copy(second_ref, new_second_ref, sems.at[3]),
    ]
    for copy in copies:
        copy.start()
    even, odd = (
        jnp.stack([dirs_ref[pair_at(pair), half] for pair in range(pairs)]).astype(jnp.float32)
        for half in range(2)
    )
    upper = halves(even.shape)
    turn = height // 2
    ordered = (
        jnp.where(upper, even, pltpu.roll(odd, turn, 1)),
        jnp.where(upper, pltpu.roll(even, turn, 1), odd),
    )
    for k in range(2):
        direction = ordered[k].astype(jnp.bfloat16).reshape(pairs * height, columns)
        update = jnp.dot(rows_ref[...], direction, preferred_element_type=jnp.float32)
        buf[k] = update.astype(buf.dtype)
        copies.append(pltpu.make_async_copy(buf.at[k], out_ref.at[k], sems.at[k]))
        copies[-1].start()
    for copy in copies:
        copy.wait()


def expand(rows, dirs, first, second):
    out_rows, rank = rows.shape
    columns = dirs.shape[-1]
    shape = (2, out_rows, columns)
    return pl.pallas_call(
        expand_kernel,
        out_shape=(
            pltpu.HBM(shape, jnp.bfloat16),
            pltpu.HBM(first.shape, first.dtype),
            pltpu.HBM(second.shape, second.dtype),
        ),
        in_specs=[VMEM] * 4,
        out_specs=[HBM] * 3,
        scratch_shapes=[pltpu.VMEM(shape, jnp.bfloat16), pltpu.SemaphoreType.DMA((4,))],
        compiler_params=PARAMS,
        cost_estimate=cost(4 * out_rows * rank * columns, 4 * out_rows * columns),
    )(rows, dirs, first, second)


def per_device(inputs, out_grads, projector, first_moment, second_moment):
    n_dp, n_tensor = lax.axis_size("dp"), lax.axis_size("tensor")
    columns = out_grads.shape[2]
    first_core = lax.axis_index("tensor") % CORES == 0
    parts, rows = low_parts(first_core, inputs, projector, n_tensor, n_dp)
    by_tensor = tensor_order(n_tensor)
    low = exchange(spread(exchange(parts, "tensor", by_tensor)), "tensor", by_tensor)
    sent = project(low, out_grads.transpose(0, 2, 1))
    own = lax.cond(
        first_core,
        scatter_by_axis,
        scatter_at_once,
        sent.reshape(n_dp, -1, columns),
    )
    direction, new_first, new_second = adam(own, first_moment, second_moment, n_dp)
    every = exchange(direction, "dp", dp_order(n_dp)).reshape(sent.shape)
    return expand(rows, every, new_first, new_second)


def solution(mesh):
    return jax.shard_map(
        per_device,
        mesh=mesh,
        in_specs=(
            P("dp", "tensor"),
            P(None, "dp", "tensor"),
            P(),
            P(None, "dp", "tensor"),
            P(None, "dp", "tensor"),
        ),
        out_specs=(P(None, "dp", "tensor"), P(None, "dp", "tensor"), P(None, "dp", "tensor")),
        check_vma=False,
    )
```

```python
import jax
import jax.numpy as jnp
from jax import lax
from jax.experimental import pallas as pl
from jax.experimental.pallas import tpu as pltpu
from jax.sharding import PartitionSpec as P

FIRST_FIX = 1.0 - 0.9**10
SECOND_FIX = 1.0 - 0.999**10
PARAMS = pltpu.CompilerParams(vmem_limit_bytes=16 * 1024 * 1024)
CHIPS_Z = 8
LAST_X, LAST_Y, LAST_Z = 2, 4, 4
CORES = 2
SMEM = pl.BlockSpec(memory_space=pltpu.SMEM)
VMEM = pl.BlockSpec(memory_space=pltpu.VMEM)
HBM = pl.BlockSpec(memory_space=pltpu.HBM)


def exchange(blocks, axis, groups=None):
    return lax.all_to_all(blocks, axis, 0, 0, axis_index_groups=groups)


def far_first(n, last):
    steps = [0, n // 2] + [sign * far for far in range(n // 2 - 1, 0, -1) for sign in (-1, 1)]
    return [(last + step) % n for step in steps]


def dp_order(n_dp):
    n_x = n_dp // CHIPS_Z
    return [x * CHIPS_Z + z for x in far_first(n_x, LAST_X) for z in far_first(CHIPS_Z, LAST_Z)]


def tensor_order(n_tensor):
    chips = far_first(n_tensor // CORES, LAST_Y)
    order = [chip * CORES + core for chip in chips for core in (1, 0)]
    return order[:1] + order[2:] + order[1:2]


def rows_sum(parts):
    return jnp.sum(parts.astype(jnp.float32), axis=0)


def scatter_at_once(sent):
    return rows_sum(exchange(sent, "dp", [dp_order(sent.shape[0])]))


def scatter_by_axis(sent):
    n_dp, height, columns = sent.shape
    n_x = n_dp // CHIPS_Z
    lines = [[x * CHIPS_Z + z for x in far_first(n_x, LAST_X)] for z in range(CHIPS_Z)]
    planes = [[x * CHIPS_Z + z for z in far_first(CHIPS_Z, LAST_Z)] for x in range(n_x)]
    along_x = exchange(sent.reshape(n_x, CHIPS_Z * height, columns), "dp", lines)
    own_plane = rows_sum(along_x).astype(sent.dtype).reshape(CHIPS_Z, height, columns)
    return rows_sum(exchange(own_plane, "dp", planes))


def cost(flops, nbytes):
    return pl.CostEstimate(flops=flops, bytes_accessed=nbytes, transcendentals=0)


def low_kernel(first_core_ref, x_ref, p_ref, parts_ref, rows_ref, x_buf, p_buf, sems):
    n, height, tokens = parts_ref.shape
    feats, out_rows = x_ref.shape[0], rows_ref.shape[0]
    chip = lax.axis_index("tensor") // CORES
    own = pl.multiple_of((chip * CORES + 1 - first_core_ref[0]) * feats, 16)
    block = pl.multiple_of(lax.axis_index("dp") * out_rows, 16)
    copies = (
        pltpu.make_async_copy(p_ref.at[pl.ds(own, feats)], p_buf, sems.at[0]),
        pltpu.make_async_copy(x_ref, x_buf, sems.at[1]),
        pltpu.make_async_copy(p_ref.at[pl.ds(block, out_rows)], rows_ref, sems.at[2]),
    )
    for copy in copies:
        copy.start()
    copies[0].wait()
    copies[1].wait()
    partial_sum = lax.dot_general(
        p_buf[...], x_buf[...], (((0,), (0,)), ((), ())), preferred_element_type=jnp.float32
    )
    parts_ref[...] = partial_sum.astype(parts_ref.dtype).reshape(n, height, tokens)
    copies[2].wait()


def low_parts(first_core, inputs, projector, n_tensor, n_dp):
    tokens, feats = inputs.shape
    width, rank = projector.shape
    bf16 = jnp.bfloat16
    return pl.pallas_call(
        low_kernel,
        out_shape=(
            pltpu.VMEM((n_tensor, rank // n_tensor, tokens), bf16),
            pltpu.VMEM((width // n_dp, rank), bf16),
        ),
        in_specs=[SMEM, HBM, HBM],
        out_specs=[VMEM, VMEM],
        scratch_shapes=[
            pltpu.VMEM((feats, tokens), bf16),
            pltpu.VMEM((feats, rank), bf16),
            pltpu.SemaphoreType.DMA((3,)),
        ],
        compiler_params=PARAMS,
        cost_estimate=cost(2 * tokens * feats * rank, 2 * feats * (tokens + rank)),
    )(
        first_core.astype(jnp.int32).reshape(1),
        pltpu.with_memory_space_constraint(inputs.T, pltpu.HBM),
        pltpu.with_memory_space_constraint(projector, pltpu.HBM),
    )


def spread_kernel(parts_ref, out_ref):
    own = jnp.sum(parts_ref[...].astype(jnp.float32), axis=0).astype(out_ref.dtype)
    out_ref[...] = jnp.broadcast_to(own[None], out_ref.shape)


def spread(parts):
    return pl.pallas_call(
        spread_kernel,
        out_shape=pltpu.VMEM(parts.shape, parts.dtype),
        in_specs=[VMEM],
        out_specs=VMEM,
        compiler_params=PARAMS,
        cost_estimate=cost(parts.size, 4 * parts.size),
    )(parts)


def halves(shape):
    return lax.broadcasted_iota(jnp.int32, shape, 1) < shape[1] // 2


def project_kernel(low_ref, grads_ref, out_ref):
    groups, height, tokens = low_ref.shape
    columns = grads_ref.shape[1]
    low = low_ref[...].reshape(groups * height, tokens)
    gate, up = (
        lax.dot_general(
            low, grads_ref[k], (((1,), (1,)), ((), ())), preferred_element_type=jnp.float32
        ).reshape(groups, height, columns)
        for k in range(2)
    )
    upper = halves(gate.shape)
    turn = height // 2
    even = jnp.where(upper, gate, pltpu.roll(up, turn, 1)).astype(out_ref.dtype)
    odd = jnp.where(upper, pltpu.roll(gate, turn, 1), up).astype(out_ref.dtype)
    order = dp_order(2 * groups)
    for pair in range(groups):
        out_ref[order.index(2 * pair)] = even[pair]
        out_ref[order.index(2 * pair + 1)] = odd[pair]


def project(low, grads):
    groups, height, tokens = low.shape
    columns = grads.shape[1]
    return pl.pallas_call(
        project_kernel,
        out_shape=pltpu.VMEM((2 * groups, height, columns), jnp.bfloat16),
        in_specs=[VMEM, VMEM],
        out_specs=VMEM,
        compiler_params=PARAMS,
        cost_estimate=cost(4 * groups * height * tokens * columns, 4 * tokens * columns),
    )(low, grads)


def adam_kernel(own_ref, first_ref, second_ref, out_ref, new_first_ref, new_second_ref):
    n_grads, height, _ = first_ref.shape
    direction = []
    for k in range(n_grads):
        projected = own_ref[k * height : (k + 1) * height]
        first = 0.9 * first_ref[k] + 0.1 * projected
        second = 0.999 * second_ref[k] + 0.001 * projected * projected
        new_first_ref[k] = first
        new_second_ref[k] = second
        direction.append(first / FIRST_FIX / (jnp.sqrt(second / SECOND_FIX) + 1e-08))
    direction = jnp.concatenate(direction, axis=0).astype(out_ref.dtype)
    out_ref[...] = jnp.broadcast_to(direction[None], out_ref.shape)


def adam(own, first, second, n_dp):
    return pl.pallas_call(
        adam_kernel,
        out_shape=(
            pltpu.VMEM((n_dp, *own.shape), jnp.bfloat16),
            pltpu.VMEM(first.shape, jnp.float32),
            pltpu.VMEM(second.shape, jnp.float32),
        ),
        in_specs=[VMEM] * 3,
        out_specs=[VMEM] * 3,
        compiler_params=PARAMS,
        cost_estimate=cost(20 * own.size, 2 * n_dp * own.size),
    )(own, first, second)


def expand_kernel(
    rows_ref, dirs_ref, first_ref, second_ref, out_ref, new_first_ref, new_second_ref, buf, sems
):
    n_dp, height, columns = dirs_ref.shape
    order = dp_order(n_dp)
    copies = [
        pltpu.make_async_copy(first_ref, new_first_ref, sems.at[2]),
        pltpu.make_async_copy(second_ref, new_second_ref, sems.at[3]),
    ]
    for copy in copies:
        copy.start()
    even, odd = (
        jnp.stack([dirs_ref[order.index(at)] for at in range(half, n_dp, 2)]).astype(jnp.float32)
        for half in range(2)
    )
    upper = halves(even.shape)
    turn = height // 2
    ordered = (
        jnp.where(upper, even, pltpu.roll(odd, turn, 1)),
        jnp.where(upper, pltpu.roll(even, turn, 1), odd),
    )
    for k in range(2):
        direction = ordered[k].astype(jnp.bfloat16).reshape(n_dp // 2 * height, columns)
        update = jnp.dot(rows_ref[...], direction, preferred_element_type=jnp.float32)
        buf[k] = update.astype(buf.dtype)
        copies.append(pltpu.make_async_copy(buf.at[k], out_ref.at[k], sems.at[k]))
        copies[-1].start()
    for copy in copies:
        copy.wait()


def expand(rows, dirs, first, second):
    out_rows, rank = rows.shape
    columns = dirs.shape[-1]
    shape = (2, out_rows, columns)
    return pl.pallas_call(
        expand_kernel,
        out_shape=(
            pltpu.HBM(shape, jnp.bfloat16),
            pltpu.HBM(first.shape, first.dtype),
            pltpu.HBM(second.shape, second.dtype),
        ),
        in_specs=[VMEM] * 4,
        out_specs=[HBM] * 3,
        scratch_shapes=[pltpu.VMEM(shape, jnp.bfloat16), pltpu.SemaphoreType.DMA((4,))],
        compiler_params=PARAMS,
        cost_estimate=cost(4 * out_rows * rank * columns, 4 * out_rows * columns),
    )(rows, dirs, first, second)


def per_device(inputs, out_grads, projector, first_moment, second_moment):
    n_dp, n_tensor = lax.axis_size("dp"), lax.axis_size("tensor")
    first_core = lax.axis_index("tensor") % CORES == 0
    parts, rows = low_parts(first_core, inputs, projector, n_tensor, n_dp)
    by_tensor = [tensor_order(n_tensor)]
    low = exchange(spread(exchange(parts, "tensor", by_tensor)), "tensor", by_tensor)
    sent = project(low, out_grads.transpose(0, 2, 1))
    own = lax.cond(first_core, scatter_by_axis, scatter_at_once, sent)
    direction, new_first, new_second = adam(own, first_moment, second_moment, n_dp)
    every = exchange(direction, "dp", [dp_order(n_dp)])
    return expand(rows, every, new_first, new_second)


def solution(mesh):
    return jax.shard_map(
        per_device,
        mesh=mesh,
        in_specs=(
            P("dp", "tensor"),
            P(None, "dp", "tensor"),
            P(),
            P(None, "dp", "tensor"),
            P(None, "dp", "tensor"),
        ),
        out_specs=(P(None, "dp", "tensor"), P(None, "dp", "tensor"), P(None, "dp", "tensor")),
        check_vma=False,
    )
```

```python
import jax
import jax.numpy as jnp
from jax import lax
from jax.experimental import pallas as pl
from jax.experimental.pallas import tpu as pltpu
from jax.sharding import PartitionSpec as P

FIRST_FIX = 1.0 - 0.9**10
SECOND_FIX = 1.0 - 0.999**10
PARAMS = pltpu.CompilerParams(vmem_limit_bytes=16 * 1024 * 1024)
CHIPS_Z = 8
LAST_X, LAST_Y, LAST_Z = 2, 4, 4
CORES = 2
SMEM = pl.BlockSpec(memory_space=pltpu.SMEM)
VMEM = pl.BlockSpec(memory_space=pltpu.VMEM)
HBM = pl.BlockSpec(memory_space=pltpu.HBM)


def exchange(blocks, axis, groups=None):
    return lax.all_to_all(blocks, axis, 0, 0, axis_index_groups=groups)


def far_first(n, last):
    steps = [0, n // 2] + [sign * far for far in range(n // 2 - 1, 0, -1) for sign in (-1, 1)]
    return [(last + step) % n for step in steps]


def dp_order(n_dp):
    n_x = n_dp // CHIPS_Z
    return [x * CHIPS_Z + z for x in far_first(n_x, LAST_X) for z in far_first(CHIPS_Z, LAST_Z)]


def tensor_order(n_tensor):
    chips = far_first(n_tensor // CORES, LAST_Y)
    order = [chip * CORES + core for chip in chips for core in (1, 0)]
    return order[:1] + order[2:] + order[1:2]


def rows_sum(parts):
    return jnp.sum(parts.astype(jnp.float32), axis=0)


def scatter_at_once(sent):
    return rows_sum(exchange(sent, "dp", [dp_order(sent.shape[0])]))


def scatter_by_axis(sent):
    n_dp, own_rank, width = sent.shape
    n_x = n_dp // CHIPS_Z
    lines = [[x * CHIPS_Z + z for x in far_first(n_x, LAST_X)] for z in range(CHIPS_Z)]
    planes = [[x * CHIPS_Z + z for z in far_first(CHIPS_Z, LAST_Z)] for x in range(n_x)]
    along_x = exchange(sent.reshape(n_x, CHIPS_Z, own_rank, width), "dp", lines)
    return rows_sum(exchange(rows_sum(along_x).astype(sent.dtype), "dp", planes))


def cost(flops, nbytes):
    return pl.CostEstimate(flops=flops, bytes_accessed=nbytes, transcendentals=0)


def low_kernel(first_core_ref, x_ref, p_ref, parts_ref, rows_ref, x_buf, p_buf, sems):
    n, height, tokens = parts_ref.shape
    feats, out_rows = x_ref.shape[0], rows_ref.shape[0]
    chip = lax.axis_index("tensor") // CORES
    own = pl.multiple_of((chip * CORES + 1 - first_core_ref[0]) * feats, 16)
    block = pl.multiple_of(lax.axis_index("dp") * out_rows, 16)
    copies = (
        pltpu.make_async_copy(p_ref.at[pl.ds(own, feats)], p_buf, sems.at[0]),
        pltpu.make_async_copy(x_ref, x_buf, sems.at[1]),
        pltpu.make_async_copy(p_ref.at[pl.ds(block, out_rows)], rows_ref, sems.at[2]),
    )
    for copy in copies:
        copy.start()
    copies[0].wait()
    copies[1].wait()
    partial_sum = lax.dot_general(
        p_buf[...], x_buf[...], (((0,), (0,)), ((), ())), preferred_element_type=jnp.float32
    )
    parts_ref[...] = partial_sum.astype(parts_ref.dtype).reshape(n, height, tokens)
    copies[2].wait()


def low_parts(first_core, inputs, projector, n_tensor, n_dp):
    tokens, feats = inputs.shape
    width, rank = projector.shape
    bf16 = jnp.bfloat16
    return pl.pallas_call(
        low_kernel,
        out_shape=(
            pltpu.VMEM((n_tensor, rank // n_tensor, tokens), bf16),
            pltpu.VMEM((width // n_dp, rank), bf16),
        ),
        in_specs=[SMEM, HBM, HBM],
        out_specs=[VMEM, VMEM],
        scratch_shapes=[
            pltpu.VMEM((feats, tokens), bf16),
            pltpu.VMEM((feats, rank), bf16),
            pltpu.SemaphoreType.DMA((3,)),
        ],
        compiler_params=PARAMS,
        cost_estimate=cost(2 * tokens * feats * rank, 2 * feats * (tokens + rank)),
    )(
        first_core.astype(jnp.int32).reshape(1),
        pltpu.with_memory_space_constraint(inputs.T, pltpu.HBM),
        pltpu.with_memory_space_constraint(projector, pltpu.HBM),
    )


def spread_kernel(parts_ref, out_ref):
    own = jnp.sum(parts_ref[...].astype(jnp.float32), axis=0).astype(out_ref.dtype)
    out_ref[...] = jnp.broadcast_to(own[None], out_ref.shape)


def spread(parts):
    return pl.pallas_call(
        spread_kernel,
        out_shape=pltpu.VMEM(parts.shape, parts.dtype),
        in_specs=[VMEM],
        out_specs=VMEM,
        compiler_params=PARAMS,
        cost_estimate=cost(parts.size, 4 * parts.size),
    )(parts)


def project_kernel(low_ref, grads_ref, out_ref):
    groups, height, tokens = low_ref.shape
    n_grads, columns, _ = grads_ref.shape
    n_dp, own_rank, _ = out_ref.shape
    projected = lax.dot_general(
        low_ref[...].reshape(groups * height, tokens),
        grads_ref[...].reshape(n_grads * columns, tokens),
        (((1,), (1,)), ((), ())),
        preferred_element_type=jnp.float32,
    )
    order = dp_order(n_dp)
    for at in range(n_dp):
        rows = projected[at * own_rank : (at + 1) * own_rank]
        out_ref[order.index(at)] = rows.astype(out_ref.dtype)


def project(low, grads, n_dp):
    groups, height, tokens = low.shape
    n_grads, columns, _ = grads.shape
    rank = groups * height
    return pl.pallas_call(
        project_kernel,
        out_shape=pltpu.VMEM((n_dp, rank // n_dp, n_grads * columns), jnp.bfloat16),
        in_specs=[VMEM, VMEM],
        out_specs=VMEM,
        compiler_params=PARAMS,
        cost_estimate=cost(2 * rank * tokens * n_grads * columns, 4 * tokens * columns),
    )(low, grads)


def adam_kernel(own_ref, first_ref, second_ref, out_ref, new_first_ref, new_second_ref):
    n_grads, _, columns = first_ref.shape
    direction = []
    for k in range(n_grads):
        projected = own_ref[:, k * columns : (k + 1) * columns]
        first = 0.9 * first_ref[k] + 0.1 * projected
        second = 0.999 * second_ref[k] + 0.001 * projected * projected
        new_first_ref[k] = first
        new_second_ref[k] = second
        direction.append(first / FIRST_FIX / (jnp.sqrt(second / SECOND_FIX) + 1e-08))
    direction = jnp.concatenate(direction, axis=1).astype(out_ref.dtype)
    out_ref[...] = jnp.broadcast_to(direction[None], out_ref.shape)


def adam(own, first, second, n_dp):
    return pl.pallas_call(
        adam_kernel,
        out_shape=(
            pltpu.VMEM((n_dp, *own.shape), jnp.bfloat16),
            pltpu.VMEM(first.shape, jnp.float32),
            pltpu.VMEM(second.shape, jnp.float32),
        ),
        in_specs=[VMEM] * 3,
        out_specs=[VMEM] * 3,
        compiler_params=PARAMS,
        cost_estimate=cost(20 * own.size, 2 * n_dp * own.size),
    )(own, first, second)


def expand_kernel(
    rows_ref, dirs_ref, first_ref, second_ref, out_ref, new_first_ref, new_second_ref, buf, sems
):
    n_dp, columns = dirs_ref.shape[0], out_ref.shape[2]
    order = dp_order(n_dp)
    copies = [
        pltpu.make_async_copy(first_ref, new_first_ref, sems.at[2]),
        pltpu.make_async_copy(second_ref, new_second_ref, sems.at[3]),
    ]
    for copy in copies:
        copy.start()
    direction = jnp.concatenate(
        [dirs_ref[order.index(at)].astype(jnp.float32) for at in range(n_dp)], axis=0
    ).astype(jnp.bfloat16)
    update = jnp.dot(rows_ref[...], direction, preferred_element_type=jnp.float32)
    update = update.astype(buf.dtype)
    for k in range(2):
        buf[k] = update[:, k * columns : (k + 1) * columns]
        copies.append(pltpu.make_async_copy(buf.at[k], out_ref.at[k], sems.at[k]))
        copies[-1].start()
    for copy in copies:
        copy.wait()


def expand(rows, dirs, first, second):
    out_rows, rank = rows.shape
    columns = dirs.shape[-1] // 2
    shape = (2, out_rows, columns)
    return pl.pallas_call(
        expand_kernel,
        out_shape=(
            pltpu.HBM(shape, jnp.bfloat16),
            pltpu.HBM(first.shape, first.dtype),
            pltpu.HBM(second.shape, second.dtype),
        ),
        in_specs=[VMEM] * 4,
        out_specs=[HBM] * 3,
        scratch_shapes=[pltpu.VMEM(shape, jnp.bfloat16), pltpu.SemaphoreType.DMA((4,))],
        compiler_params=PARAMS,
        cost_estimate=cost(4 * out_rows * rank * columns, 4 * out_rows * columns),
    )(rows, dirs, first, second)


def per_device(inputs, out_grads, projector, first_moment, second_moment):
    n_dp, n_tensor = lax.axis_size("dp"), lax.axis_size("tensor")
    first_core = lax.axis_index("tensor") % CORES == 0
    parts, rows = low_parts(first_core, inputs, projector, n_tensor, n_dp)
    by_tensor = [tensor_order(n_tensor)]
    low = exchange(spread(exchange(parts, "tensor", by_tensor)), "tensor", by_tensor)
    sent = project(low, out_grads.transpose(0, 2, 1), n_dp)
    own = lax.cond(first_core, scatter_by_axis, scatter_at_once, sent)
    direction, new_first, new_second = adam(own, first_moment, second_moment, n_dp)
    every = exchange(direction, "dp", [dp_order(n_dp)])
    return expand(rows, every, new_first, new_second)


def solution(mesh):
    return jax.shard_map(
        per_device,
        mesh=mesh,
        in_specs=(
            P("dp", "tensor"),
            P(None, "dp", "tensor"),
            P(),
            P(None, "dp", "tensor"),
            P(None, "dp", "tensor"),
        ),
        out_specs=(P(None, "dp", "tensor"), P(None, "dp", "tensor"), P(None, "dp", "tensor")),
        check_vma=False,
    )
```

```python
import jax
import jax.numpy as jnp
from jax import lax
from jax.experimental import pallas as pl
from jax.experimental.pallas import tpu as pltpu
from jax.sharding import PartitionSpec as P

FIRST_FIX = 1.0 - 0.9**10
SECOND_FIX = 1.0 - 0.999**10
PARAMS = pltpu.CompilerParams(vmem_limit_bytes=16 * 1024 * 1024)
CHIPS_Z = 8
LAST_X, LAST_Y, LAST_Z = 2, 4, 4
CORES = 2
SMEM = pl.BlockSpec(memory_space=pltpu.SMEM)
VMEM = pl.BlockSpec(memory_space=pltpu.VMEM)
HBM = pl.BlockSpec(memory_space=pltpu.HBM)


def exchange(blocks, axis, groups=None):
    return lax.all_to_all(blocks, axis, 0, 0, axis_index_groups=groups)


def far_first(n, last):
    steps = [0, n // 2] + [sign * far for far in range(n // 2 - 1, 0, -1) for sign in (-1, 1)]
    return [(last + step) % n for step in steps]


def dp_order(n_dp):
    n_x = n_dp // CHIPS_Z
    return [x * CHIPS_Z + z for x in far_first(n_x, LAST_X) for z in far_first(CHIPS_Z, LAST_Z)]


def tensor_order(n_tensor):
    chips = far_first(n_tensor // CORES, LAST_Y)
    order = [chip * CORES + core for chip in chips for core in (1, 0)]
    return order[:1] + order[2:] + order[1:2]


def rows_sum(parts):
    return jnp.sum(parts.astype(jnp.float32), axis=0)


def scatter_at_once(sent):
    return rows_sum(exchange(sent, "dp", [dp_order(sent.shape[0])]))


def scatter_by_axis(sent):
    n_dp, own_rank, width = sent.shape
    n_x = n_dp // CHIPS_Z
    lines = [[x * CHIPS_Z + z for x in far_first(n_x, LAST_X)] for z in range(CHIPS_Z)]
    planes = [[x * CHIPS_Z + z for z in far_first(CHIPS_Z, LAST_Z)] for x in range(n_x)]
    along_x = exchange(sent.reshape(n_x, CHIPS_Z, own_rank, width), "dp", lines)
    return rows_sum(exchange(total(along_x), "dp", planes))


def cost(flops, nbytes):
    return pl.CostEstimate(flops=flops, bytes_accessed=nbytes, transcendentals=0)


def low_kernel(first_core_ref, x_ref, p_ref, parts_ref, rows_ref, x_buf, p_buf, sems):
    n, height, tokens = parts_ref.shape
    feats, out_rows = x_ref.shape[0], rows_ref.shape[0]
    chip = lax.axis_index("tensor") // CORES
    own = pl.multiple_of((chip * CORES + 1 - first_core_ref[0]) * feats, 16)
    block = pl.multiple_of(lax.axis_index("dp") * out_rows, 16)
    copies = (
        pltpu.make_async_copy(p_ref.at[pl.ds(own, feats)], p_buf, sems.at[0]),
        pltpu.make_async_copy(x_ref, x_buf, sems.at[1]),
        pltpu.make_async_copy(p_ref.at[pl.ds(block, out_rows)], rows_ref, sems.at[2]),
    )
    for copy in copies:
        copy.start()
    copies[0].wait()
    copies[1].wait()
    partial_sum = lax.dot_general(
        p_buf[...], x_buf[...], (((0,), (0,)), ((), ())), preferred_element_type=jnp.float32
    )
    parts_ref[...] = partial_sum.astype(parts_ref.dtype).reshape(n, height, tokens)
    copies[2].wait()


def low_parts(first_core, inputs, projector, n_tensor, n_dp):
    tokens, feats = inputs.shape
    width, rank = projector.shape
    bf16 = jnp.bfloat16
    return pl.pallas_call(
        low_kernel,
        out_shape=(
            pltpu.VMEM((n_tensor, rank // n_tensor, tokens), bf16),
            pltpu.VMEM((width // n_dp, rank), bf16),
        ),
        in_specs=[SMEM, HBM, HBM],
        out_specs=[VMEM, VMEM],
        scratch_shapes=[
            pltpu.VMEM((feats, tokens), bf16),
            pltpu.VMEM((feats, rank), bf16),
            pltpu.SemaphoreType.DMA((3,)),
        ],
        compiler_params=PARAMS,
        cost_estimate=cost(2 * tokens * feats * rank, 2 * feats * (tokens + rank)),
    )(
        first_core.astype(jnp.int32).reshape(1),
        pltpu.with_memory_space_constraint(inputs.T, pltpu.HBM),
        pltpu.with_memory_space_constraint(projector, pltpu.HBM),
    )


def total_kernel(parts_ref, out_ref):
    out_ref[...] = rows_sum(parts_ref[...]).astype(out_ref.dtype)


def total(parts):
    return pl.pallas_call(
        total_kernel,
        out_shape=pltpu.VMEM(parts.shape[1:], parts.dtype),
        in_specs=[VMEM],
        out_specs=VMEM,
        compiler_params=PARAMS,
        cost_estimate=cost(parts.size, 3 * parts.size),
    )(parts)


def spread_kernel(parts_ref, out_ref):
    own = jnp.sum(parts_ref[...].astype(jnp.float32), axis=0).astype(out_ref.dtype)
    out_ref[...] = jnp.broadcast_to(own[None], out_ref.shape)


def spread(parts):
    return pl.pallas_call(
        spread_kernel,
        out_shape=pltpu.VMEM(parts.shape, parts.dtype),
        in_specs=[VMEM],
        out_specs=VMEM,
        compiler_params=PARAMS,
        cost_estimate=cost(parts.size, 4 * parts.size),
    )(parts)


def project_kernel(low_ref, grads_ref, out_ref):
    groups, height, tokens = low_ref.shape
    n_grads, columns, _ = grads_ref.shape
    n_dp, own_rank, _ = out_ref.shape
    projected = lax.dot_general(
        low_ref[...].reshape(groups * height, tokens),
        grads_ref[...].reshape(n_grads * columns, tokens),
        (((1,), (1,)), ((), ())),
        preferred_element_type=jnp.float32,
    )
    order = dp_order(n_dp)
    for at in range(n_dp):
        rows = projected[at * own_rank : (at + 1) * own_rank]
        out_ref[order.index(at)] = rows.astype(out_ref.dtype)


def project(low, grads, n_dp):
    groups, height, tokens = low.shape
    n_grads, columns, _ = grads.shape
    rank = groups * height
    return pl.pallas_call(
        project_kernel,
        out_shape=pltpu.VMEM((n_dp, rank // n_dp, n_grads * columns), jnp.bfloat16),
        in_specs=[VMEM, VMEM],
        out_specs=VMEM,
        compiler_params=PARAMS,
        cost_estimate=cost(2 * rank * tokens * n_grads * columns, 4 * tokens * columns),
    )(low, grads)


def adam_kernel(own_ref, first_ref, second_ref, out_ref, new_first_ref, new_second_ref):
    n_grads, _, columns = first_ref.shape
    direction = []
    for k in range(n_grads):
        projected = own_ref[:, k * columns : (k + 1) * columns]
        first = 0.9 * first_ref[k] + 0.1 * projected
        second = 0.999 * second_ref[k] + 0.001 * projected * projected
        new_first_ref[k] = first
        new_second_ref[k] = second
        direction.append(first / FIRST_FIX / (jnp.sqrt(second / SECOND_FIX) + 1e-08))
    direction = jnp.concatenate(direction, axis=1).astype(out_ref.dtype)
    out_ref[...] = jnp.broadcast_to(direction[None], out_ref.shape)


def adam(own, first, second, n_dp):
    return pl.pallas_call(
        adam_kernel,
        out_shape=(
            pltpu.VMEM((n_dp, *own.shape), jnp.bfloat16),
            pltpu.VMEM(first.shape, jnp.float32),
            pltpu.VMEM(second.shape, jnp.float32),
        ),
        in_specs=[VMEM] * 3,
        out_specs=[VMEM] * 3,
        compiler_params=PARAMS,
        cost_estimate=cost(20 * own.size, 2 * n_dp * own.size),
    )(own, first, second)


def expand_kernel(
    rows_ref, dirs_ref, first_ref, second_ref, out_ref, new_first_ref, new_second_ref, buf, sems
):
    n_dp, columns = dirs_ref.shape[0], out_ref.shape[2]
    order = dp_order(n_dp)
    copies = [
        pltpu.make_async_copy(first_ref, new_first_ref, sems.at[2]),
        pltpu.make_async_copy(second_ref, new_second_ref, sems.at[3]),
    ]
    for copy in copies:
        copy.start()
    direction = jnp.concatenate(
        [dirs_ref[order.index(at)].astype(jnp.float32) for at in range(n_dp)], axis=0
    ).astype(jnp.bfloat16)
    update = jnp.dot(rows_ref[...], direction, preferred_element_type=jnp.float32)
    update = update.astype(buf.dtype)
    for k in range(2):
        buf[k] = update[:, k * columns : (k + 1) * columns]
        copies.append(pltpu.make_async_copy(buf.at[k], out_ref.at[k], sems.at[k]))
        copies[-1].start()
    for copy in copies:
        copy.wait()


def expand(rows, dirs, first, second):
    out_rows, rank = rows.shape
    columns = dirs.shape[-1] // 2
    shape = (2, out_rows, columns)
    return pl.pallas_call(
        expand_kernel,
        out_shape=(
            pltpu.HBM(shape, jnp.bfloat16),
            pltpu.HBM(first.shape, first.dtype),
            pltpu.HBM(second.shape, second.dtype),
        ),
        in_specs=[VMEM] * 4,
        out_specs=[HBM] * 3,
        scratch_shapes=[pltpu.VMEM(shape, jnp.bfloat16), pltpu.SemaphoreType.DMA((4,))],
        compiler_params=PARAMS,
        cost_estimate=cost(4 * out_rows * rank * columns, 4 * out_rows * columns),
    )(rows, dirs, first, second)


def per_device(inputs, out_grads, projector, first_moment, second_moment):
    n_dp, n_tensor = lax.axis_size("dp"), lax.axis_size("tensor")
    first_core = lax.axis_index("tensor") % CORES == 0
    parts, rows = low_parts(first_core, inputs, projector, n_tensor, n_dp)
    by_tensor = [tensor_order(n_tensor)]
    low = exchange(spread(exchange(parts, "tensor", by_tensor)), "tensor", by_tensor)
    sent = project(low, out_grads.transpose(0, 2, 1), n_dp)
    own = lax.cond(first_core, scatter_by_axis, scatter_at_once, sent)
    direction, new_first, new_second = adam(own, first_moment, second_moment, n_dp)
    every = exchange(direction, "dp", [dp_order(n_dp)])
    return expand(rows, every, new_first, new_second)


def solution(mesh):
    return jax.shard_map(
        per_device,
        mesh=mesh,
        in_specs=(
            P("dp", "tensor"),
            P(None, "dp", "tensor"),
            P(),
            P(None, "dp", "tensor"),
            P(None, "dp", "tensor"),
        ),
        out_specs=(P(None, "dp", "tensor"), P(None, "dp", "tensor"), P(None, "dp", "tensor")),
        check_vma=False,
    )
```

```python
import jax
import jax.numpy as jnp
from jax import lax
from jax.experimental import pallas as pl
from jax.experimental.pallas import tpu as pltpu
from jax.sharding import PartitionSpec as P

FIRST_FIX = 1.0 - 0.9**10
SECOND_FIX = 1.0 - 0.999**10
PARAMS = pltpu.CompilerParams(vmem_limit_bytes=16 * 1024 * 1024)
CHIPS_Z = 8
LAST_X, LAST_Y, LAST_Z = 2, 4, 6
CORES = 2
SMEM = pl.BlockSpec(memory_space=pltpu.SMEM)
VMEM = pl.BlockSpec(memory_space=pltpu.VMEM)
HBM = pl.BlockSpec(memory_space=pltpu.HBM)


def exchange(blocks, axis, groups=None):
    return lax.all_to_all(blocks, axis, 0, 0, axis_index_groups=groups)


def far_first(n, last):
    steps = [0, n // 2] + [sign * far for far in range(n // 2 - 1, 0, -1) for sign in (-1, 1)]
    return [(last + step) % n for step in steps]


def dp_order(n_dp):
    n_x = n_dp // CHIPS_Z
    return [x * CHIPS_Z + z for x in far_first(n_x, LAST_X) for z in far_first(CHIPS_Z, LAST_Z)]


def tensor_order(n_tensor):
    chips = far_first(n_tensor // CORES, LAST_Y)
    order = [chip * CORES + core for chip in chips for core in (1, 0)]
    return order[:1] + order[2:] + order[1:2]


def rows_sum(parts):
    return jnp.sum(parts.astype(jnp.float32), axis=0)


def scatter_at_once(sent):
    return rows_sum(exchange(sent, "dp", [dp_order(sent.shape[0])]))


def scatter_by_axis(sent):
    n_dp, own_rank, width = sent.shape
    n_x = n_dp // CHIPS_Z
    lines = [[x * CHIPS_Z + z for x in far_first(n_x, LAST_X)] for z in range(CHIPS_Z)]
    planes = [[x * CHIPS_Z + z for z in far_first(CHIPS_Z, LAST_Z)] for x in range(n_x)]
    along_x = exchange(sent.reshape(n_x, CHIPS_Z, own_rank, width), "dp", lines)
    return rows_sum(exchange(total(along_x), "dp", planes))


def cost(flops, nbytes):
    return pl.CostEstimate(flops=flops, bytes_accessed=nbytes, transcendentals=0)


def low_kernel(first_core_ref, x_ref, p_ref, parts_ref, rows_ref, x_buf, p_buf, sems):
    n, height, tokens = parts_ref.shape
    feats, out_rows = x_ref.shape[0], rows_ref.shape[0]
    chip = lax.axis_index("tensor") // CORES
    own = pl.multiple_of((chip * CORES + 1 - first_core_ref[0]) * feats, 16)
    block = pl.multiple_of(lax.axis_index("dp") * out_rows, 16)
    copies = (
        pltpu.make_async_copy(p_ref.at[pl.ds(own, feats)], p_buf, sems.at[0]),
        pltpu.make_async_copy(x_ref, x_buf, sems.at[1]),
        pltpu.make_async_copy(p_ref.at[pl.ds(block, out_rows)], rows_ref, sems.at[2]),
    )
    for copy in copies:
        copy.start()
    copies[0].wait()
    copies[1].wait()
    partial_sum = lax.dot_general(
        p_buf[...], x_buf[...], (((0,), (0,)), ((), ())), preferred_element_type=jnp.float32
    )
    parts_ref[...] = partial_sum.astype(parts_ref.dtype).reshape(n, height, tokens)
    copies[2].wait()


def low_parts(first_core, inputs, projector, n_tensor, n_dp):
    tokens, feats = inputs.shape
    width, rank = projector.shape
    bf16 = jnp.bfloat16
    return pl.pallas_call(
        low_kernel,
        out_shape=(
            pltpu.VMEM((n_tensor, rank // n_tensor, tokens), bf16),
            pltpu.VMEM((width // n_dp, rank), bf16),
        ),
        in_specs=[SMEM, HBM, HBM],
        out_specs=[VMEM, VMEM],
        scratch_shapes=[
            pltpu.VMEM((feats, tokens), bf16),
            pltpu.VMEM((feats, rank), bf16),
            pltpu.SemaphoreType.DMA((3,)),
        ],
        compiler_params=PARAMS,
        cost_estimate=cost(2 * tokens * feats * rank, 2 * feats * (tokens + rank)),
    )(
        first_core.astype(jnp.int32).reshape(1),
        pltpu.with_memory_space_constraint(inputs.T, pltpu.HBM),
        pltpu.with_memory_space_constraint(projector, pltpu.HBM),
    )


def total_kernel(parts_ref, out_ref):
    out_ref[...] = rows_sum(parts_ref[...]).astype(out_ref.dtype)


def total(parts):
    return pl.pallas_call(
        total_kernel,
        out_shape=pltpu.VMEM(parts.shape[1:], parts.dtype),
        in_specs=[VMEM],
        out_specs=VMEM,
        compiler_params=PARAMS,
        cost_estimate=cost(parts.size, 3 * parts.size),
    )(parts)


def spread_kernel(parts_ref, out_ref):
    own = jnp.sum(parts_ref[...].astype(jnp.float32), axis=0).astype(out_ref.dtype)
    out_ref[...] = jnp.broadcast_to(own[None], out_ref.shape)


def spread(parts):
    return pl.pallas_call(
        spread_kernel,
        out_shape=pltpu.VMEM(parts.shape, parts.dtype),
        in_specs=[VMEM],
        out_specs=VMEM,
        compiler_params=PARAMS,
        cost_estimate=cost(parts.size, 4 * parts.size),
    )(parts)


def project_kernel(low_ref, grads_ref, out_ref):
    groups, height, tokens = low_ref.shape
    n_grads, columns, _ = grads_ref.shape
    n_dp, own_rank, _ = out_ref.shape
    projected = lax.dot_general(
        low_ref[...].reshape(groups * height, tokens),
        grads_ref[...].reshape(n_grads * columns, tokens),
        (((1,), (1,)), ((), ())),
        preferred_element_type=jnp.float32,
    )
    order = dp_order(n_dp)
    for at in range(n_dp):
        rows = projected[at * own_rank : (at + 1) * own_rank]
        out_ref[order.index(at)] = rows.astype(out_ref.dtype)


def project(low, grads, n_dp):
    groups, height, tokens = low.shape
    n_grads, columns, _ = grads.shape
    rank = groups * height
    return pl.pallas_call(
        project_kernel,
        out_shape=pltpu.VMEM((n_dp, rank // n_dp, n_grads * columns), jnp.bfloat16),
        in_specs=[VMEM, VMEM],
        out_specs=VMEM,
        compiler_params=PARAMS,
        cost_estimate=cost(2 * rank * tokens * n_grads * columns, 4 * tokens * columns),
    )(low, grads)


def adam_kernel(own_ref, first_ref, second_ref, out_ref, new_first_ref, new_second_ref):
    n_grads, _, columns = first_ref.shape
    direction = []
    for k in range(n_grads):
        projected = own_ref[:, k * columns : (k + 1) * columns]
        first = 0.9 * first_ref[k] + 0.1 * projected
        second = 0.999 * second_ref[k] + 0.001 * projected * projected
        new_first_ref[k] = first
        new_second_ref[k] = second
        direction.append(first / FIRST_FIX / (jnp.sqrt(second / SECOND_FIX) + 1e-08))
    direction = jnp.concatenate(direction, axis=1).astype(out_ref.dtype)
    out_ref[...] = jnp.broadcast_to(direction[None], out_ref.shape)


def adam(own, first, second, n_dp):
    return pl.pallas_call(
        adam_kernel,
        out_shape=(
            pltpu.VMEM((n_dp, *own.shape), jnp.bfloat16),
            pltpu.VMEM(first.shape, jnp.float32),
            pltpu.VMEM(second.shape, jnp.float32),
        ),
        in_specs=[VMEM] * 3,
        out_specs=[VMEM] * 3,
        compiler_params=PARAMS,
        cost_estimate=cost(20 * own.size, 2 * n_dp * own.size),
    )(own, first, second)


def expand_kernel(
    rows_ref, dirs_ref, first_ref, second_ref, out_ref, new_first_ref, new_second_ref, buf, sems
):
    n_dp, columns = dirs_ref.shape[0], out_ref.shape[2]
    order = dp_order(n_dp)
    copies = [
        pltpu.make_async_copy(first_ref, new_first_ref, sems.at[2]),
        pltpu.make_async_copy(second_ref, new_second_ref, sems.at[3]),
    ]
    for copy in copies:
        copy.start()
    direction = jnp.concatenate(
        [dirs_ref[order.index(at)].astype(jnp.float32) for at in range(n_dp)], axis=0
    ).astype(jnp.bfloat16)
    update = jnp.dot(rows_ref[...], direction, preferred_element_type=jnp.float32)
    update = update.astype(buf.dtype)
    for k in range(2):
        buf[k] = update[:, k * columns : (k + 1) * columns]
        copies.append(pltpu.make_async_copy(buf.at[k], out_ref.at[k], sems.at[k]))
        copies[-1].start()
    for copy in copies:
        copy.wait()


def expand(rows, dirs, first, second):
    out_rows, rank = rows.shape
    columns = dirs.shape[-1] // 2
    shape = (2, out_rows, columns)
    return pl.pallas_call(
        expand_kernel,
        out_shape=(
            pltpu.HBM(shape, jnp.bfloat16),
            pltpu.HBM(first.shape, first.dtype),
            pltpu.HBM(second.shape, second.dtype),
        ),
        in_specs=[VMEM] * 4,
        out_specs=[HBM] * 3,
        scratch_shapes=[pltpu.VMEM(shape, jnp.bfloat16), pltpu.SemaphoreType.DMA((4,))],
        compiler_params=PARAMS,
        cost_estimate=cost(4 * out_rows * rank * columns, 4 * out_rows * columns),
    )(rows, dirs, first, second)


def per_device(inputs, out_grads, projector, first_moment, second_moment):
    n_dp, n_tensor = lax.axis_size("dp"), lax.axis_size("tensor")
    first_core = lax.axis_index("tensor") % CORES == 0
    parts, rows = low_parts(first_core, inputs, projector, n_tensor, n_dp)
    by_tensor = [tensor_order(n_tensor)]
    low = exchange(spread(exchange(parts, "tensor", by_tensor)), "tensor", by_tensor)
    sent = project(low, out_grads.transpose(0, 2, 1), n_dp)
    own = lax.cond(first_core, scatter_by_axis, scatter_at_once, sent)
    direction, new_first, new_second = adam(own, first_moment, second_moment, n_dp)
    every = exchange(direction, "dp", [dp_order(n_dp)])
    return expand(rows, every, new_first, new_second)


def solution(mesh):
    return jax.shard_map(
        per_device,
        mesh=mesh,
        in_specs=(
            P("dp", "tensor"),
            P(None, "dp", "tensor"),
            P(),
            P(None, "dp", "tensor"),
            P(None, "dp", "tensor"),
        ),
        out_specs=(P(None, "dp", "tensor"), P(None, "dp", "tensor"), P(None, "dp", "tensor")),
        check_vma=False,
    )
```

```python
import jax
import jax.numpy as jnp
from jax import lax
from jax.experimental import pallas as pl
from jax.experimental.pallas import tpu as pltpu
from jax.sharding import PartitionSpec as P

FIRST_FIX = 1.0 - 0.9**10
SECOND_FIX = 1.0 - 0.999**10
PARAMS = pltpu.CompilerParams(vmem_limit_bytes=16 * 1024 * 1024)
CHIPS_Z = 8
LAST_X, LAST_Y, LAST_Z = 2, 4, 6
GATHER_Z = 4
CORES = 2
SMEM = pl.BlockSpec(memory_space=pltpu.SMEM)
VMEM = pl.BlockSpec(memory_space=pltpu.VMEM)
HBM = pl.BlockSpec(memory_space=pltpu.HBM)


def exchange(blocks, axis, groups=None):
    return lax.all_to_all(blocks, axis, 0, 0, axis_index_groups=groups)


def far_first(n, last):
    steps = [0, n // 2] + [sign * far for far in range(n // 2 - 1, 0, -1) for sign in (-1, 1)]
    return [(last + step) % n for step in steps]


def dp_order(n_dp, last_z=LAST_Z):
    n_x = n_dp // CHIPS_Z
    return [x * CHIPS_Z + z for x in far_first(n_x, LAST_X) for z in far_first(CHIPS_Z, last_z)]


def tensor_order(n_tensor):
    chips = far_first(n_tensor // CORES, LAST_Y)
    order = [chip * CORES + core for chip in chips for core in (1, 0)]
    return order[:1] + order[2:] + order[1:2]


def rows_sum(parts):
    return jnp.sum(parts.astype(jnp.float32), axis=0)


def scatter_at_once(sent):
    return rows_sum(exchange(sent, "dp", [dp_order(sent.shape[0])]))


def scatter_by_axis(sent):
    n_dp, own_rank, width = sent.shape
    n_x = n_dp // CHIPS_Z
    lines = [[x * CHIPS_Z + z for x in far_first(n_x, LAST_X)] for z in range(CHIPS_Z)]
    planes = [[x * CHIPS_Z + z for z in far_first(CHIPS_Z, LAST_Z)] for x in range(n_x)]
    along_x = exchange(sent.reshape(n_x, CHIPS_Z, own_rank, width), "dp", lines)
    return rows_sum(exchange(total(along_x), "dp", planes))


def cost(flops, nbytes):
    return pl.CostEstimate(flops=flops, bytes_accessed=nbytes, transcendentals=0)


def low_kernel(first_core_ref, x_ref, p_ref, parts_ref, rows_ref, x_buf, p_buf, sems):
    n, height, tokens = parts_ref.shape
    feats, out_rows = x_ref.shape[0], rows_ref.shape[0]
    chip = lax.axis_index("tensor") // CORES
    own = pl.multiple_of((chip * CORES + 1 - first_core_ref[0]) * feats, 16)
    block = pl.multiple_of(lax.axis_index("dp") * out_rows, 16)
    copies = (
        pltpu.make_async_copy(p_ref.at[pl.ds(own, feats)], p_buf, sems.at[0]),
        pltpu.make_async_copy(x_ref, x_buf, sems.at[1]),
        pltpu.make_async_copy(p_ref.at[pl.ds(block, out_rows)], rows_ref, sems.at[2]),
    )
    for copy in copies:
        copy.start()
    copies[0].wait()
    copies[1].wait()
    partial_sum = lax.dot_general(
        p_buf[...], x_buf[...], (((0,), (0,)), ((), ())), preferred_element_type=jnp.float32
    )
    parts_ref[...] = partial_sum.astype(parts_ref.dtype).reshape(n, height, tokens)
    copies[2].wait()


def low_parts(first_core, inputs, projector, n_tensor, n_dp):
    tokens, feats = inputs.shape
    width, rank = projector.shape
    bf16 = jnp.bfloat16
    return pl.pallas_call(
        low_kernel,
        out_shape=(
            pltpu.VMEM((n_tensor, rank // n_tensor, tokens), bf16),
            pltpu.VMEM((width // n_dp, rank), bf16),
        ),
        in_specs=[SMEM, HBM, HBM],
        out_specs=[VMEM, VMEM],
        scratch_shapes=[
            pltpu.VMEM((feats, tokens), bf16),
            pltpu.VMEM((feats, rank), bf16),
            pltpu.SemaphoreType.DMA((3,)),
        ],
        compiler_params=PARAMS,
        cost_estimate=cost(2 * tokens * feats * rank, 2 * feats * (tokens + rank)),
    )(
        first_core.astype(jnp.int32).reshape(1),
        pltpu.with_memory_space_constraint(inputs.T, pltpu.HBM),
        pltpu.with_memory_space_constraint(projector, pltpu.HBM),
    )


def total_kernel(parts_ref, out_ref):
    out_ref[...] = rows_sum(parts_ref[...]).astype(out_ref.dtype)


def total(parts):
    return pl.pallas_call(
        total_kernel,
        out_shape=pltpu.VMEM(parts.shape[1:], parts.dtype),
        in_specs=[VMEM],
        out_specs=VMEM,
        compiler_params=PARAMS,
        cost_estimate=cost(parts.size, 3 * parts.size),
    )(parts)


def spread_kernel(parts_ref, out_ref):
    own = jnp.sum(parts_ref[...].astype(jnp.float32), axis=0).astype(out_ref.dtype)
    out_ref[...] = jnp.broadcast_to(own[None], out_ref.shape)


def spread(parts):
    return pl.pallas_call(
        spread_kernel,
        out_shape=pltpu.VMEM(parts.shape, parts.dtype),
        in_specs=[VMEM],
        out_specs=VMEM,
        compiler_params=PARAMS,
        cost_estimate=cost(parts.size, 4 * parts.size),
    )(parts)


def project_kernel(low_ref, grads_ref, out_ref):
    groups, height, tokens = low_ref.shape
    n_grads, columns, _ = grads_ref.shape
    n_dp, own_rank, _ = out_ref.shape
    projected = lax.dot_general(
        low_ref[...].reshape(groups * height, tokens),
        grads_ref[...].reshape(n_grads * columns, tokens),
        (((1,), (1,)), ((), ())),
        preferred_element_type=jnp.float32,
    )
    order = dp_order(n_dp)
    for at in range(n_dp):
        rows = projected[at * own_rank : (at + 1) * own_rank]
        out_ref[order.index(at)] = rows.astype(out_ref.dtype)


def project(low, grads, n_dp):
    groups, height, tokens = low.shape
    n_grads, columns, _ = grads.shape
    rank = groups * height
    return pl.pallas_call(
        project_kernel,
        out_shape=pltpu.VMEM((n_dp, rank // n_dp, n_grads * columns), jnp.bfloat16),
        in_specs=[VMEM, VMEM],
        out_specs=VMEM,
        compiler_params=PARAMS,
        cost_estimate=cost(2 * rank * tokens * n_grads * columns, 4 * tokens * columns),
    )(low, grads)


def adam_kernel(own_ref, first_ref, second_ref, out_ref, new_first_ref, new_second_ref):
    n_grads, _, columns = first_ref.shape
    direction = []
    for k in range(n_grads):
        projected = own_ref[:, k * columns : (k + 1) * columns]
        first = 0.9 * first_ref[k] + 0.1 * projected
        second = 0.999 * second_ref[k] + 0.001 * projected * projected
        new_first_ref[k] = first
        new_second_ref[k] = second
        direction.append(first / FIRST_FIX / (jnp.sqrt(second / SECOND_FIX) + 1e-08))
    direction = jnp.concatenate(direction, axis=1).astype(out_ref.dtype)
    out_ref[...] = jnp.broadcast_to(direction[None], out_ref.shape)


def adam(own, first, second, n_dp):
    return pl.pallas_call(
        adam_kernel,
        out_shape=(
            pltpu.VMEM((n_dp, *own.shape), jnp.bfloat16),
            pltpu.VMEM(first.shape, jnp.float32),
            pltpu.VMEM(second.shape, jnp.float32),
        ),
        in_specs=[VMEM] * 3,
        out_specs=[VMEM] * 3,
        compiler_params=PARAMS,
        cost_estimate=cost(20 * own.size, 2 * n_dp * own.size),
    )(own, first, second)


def expand_kernel(
    rows_ref, dirs_ref, first_ref, second_ref, out_ref, new_first_ref, new_second_ref, buf, sems
):
    n_dp, columns = dirs_ref.shape[0], out_ref.shape[2]
    order = dp_order(n_dp, GATHER_Z)
    copies = [
        pltpu.make_async_copy(first_ref, new_first_ref, sems.at[2]),
        pltpu.make_async_copy(second_ref, new_second_ref, sems.at[3]),
    ]
    for copy in copies:
        copy.start()
    direction = jnp.concatenate(
        [dirs_ref[order.index(at)].astype(jnp.float32) for at in range(n_dp)], axis=0
    ).astype(jnp.bfloat16)
    update = jnp.dot(rows_ref[...], direction, preferred_element_type=jnp.float32)
    update = update.astype(buf.dtype)
    for k in range(2):
        buf[k] = update[:, k * columns : (k + 1) * columns]
        copies.append(pltpu.make_async_copy(buf.at[k], out_ref.at[k], sems.at[k]))
        copies[-1].start()
    for copy in copies:
        copy.wait()


def expand(rows, dirs, first, second):
    out_rows, rank = rows.shape
    columns = dirs.shape[-1] // 2
    shape = (2, out_rows, columns)
    return pl.pallas_call(
        expand_kernel,
        out_shape=(
            pltpu.HBM(shape, jnp.bfloat16),
            pltpu.HBM(first.shape, first.dtype),
            pltpu.HBM(second.shape, second.dtype),
        ),
        in_specs=[VMEM] * 4,
        out_specs=[HBM] * 3,
        scratch_shapes=[pltpu.VMEM(shape, jnp.bfloat16), pltpu.SemaphoreType.DMA((4,))],
        compiler_params=PARAMS,
        cost_estimate=cost(4 * out_rows * rank * columns, 4 * out_rows * columns),
    )(rows, dirs, first, second)


def per_device(inputs, out_grads, projector, first_moment, second_moment):
    n_dp, n_tensor = lax.axis_size("dp"), lax.axis_size("tensor")
    first_core = lax.axis_index("tensor") % CORES == 0
    parts, rows = low_parts(first_core, inputs, projector, n_tensor, n_dp)
    by_tensor = [tensor_order(n_tensor)]
    low = exchange(spread(exchange(parts, "tensor", by_tensor)), "tensor", by_tensor)
    sent = project(low, out_grads.transpose(0, 2, 1), n_dp)
    own = lax.cond(first_core, scatter_by_axis, scatter_at_once, sent)
    direction, new_first, new_second = adam(own, first_moment, second_moment, n_dp)
    every = exchange(direction, "dp", [dp_order(n_dp, GATHER_Z)])
    return expand(rows, every, new_first, new_second)


def solution(mesh):
    return jax.shard_map(
        per_device,
        mesh=mesh,
        in_specs=(
            P("dp", "tensor"),
            P(None, "dp", "tensor"),
            P(),
            P(None, "dp", "tensor"),
            P(None, "dp", "tensor"),
        ),
        out_specs=(P(None, "dp", "tensor"), P(None, "dp", "tensor"), P(None, "dp", "tensor")),
        check_vma=False,
    )
```
